32 devices in a mesh: grp: 4 (over y, x), col: 8 (over z, core).
Axes of the slice: x: 2, y: 2, z: 4, core: 2. Of those that a mesh axis runs over, the one named last changes fastest.
Arguments:
- inputs: bfloat16 [24, 256, 8192], P('grp', 'col'), may hold values from -6 to 6
- out_grads: bfloat16 [24, 256, 8192], P('grp', None, 'col'), may hold values from -0.5 to 0.5
- first_moment: float32 [8192, 8192], P(None, 'col'), may hold values from -2 to 2
- second_moment: float32 [8192, 8192], P(None, 'col'), may hold values from 0.01 to 1
- signs_in: int32 [8192], replicated, may hold values from 0 to 1
- signs_out: int32 [8192], replicated, may hold values from 0 to 1
- rows_in: int32 [64], replicated, may hold values from 0 to 8191, as said below
- rows_out: int32 [128], replicated, may hold values from 0 to 8191, as said below
- task_ids: int32 [24], P('grp'), may hold values from 0 to 7
- weights: int32 [24], P('grp'), may hold values from 1 to 4
Outputs:
- prototypes: float32 [8, 64, 128], P('grp', 'col')
The draws below stay inside these ranges and needn't reach their ends.
Inputs may be any that keep to these rules, and one draw needn't show every extreme that they name: `rows_in`: distinct row numbers. `rows_out`: distinct row numbers.
All inputs are finite; a program needn't handle non-finite values.
Results may differ from the reference program's by a relative error of at most 0.0019.
Values may be sent and summed in bfloat16 or wider, within the bound.
No kernel may reach another device: no remote copies, remote signals or barrier semaphores. Data moves between devices by JAX's collectives and lax.ppermute only.
A program may use at most 256 MiB of HBM per device.

```python
import math
import jax
import jax.numpy as jnp
from jax import lax

D = 8192
TOK = 256
R1 = 64
R2 = 128
EXAMPLES = 24
NPROTO = 8


def draw_rows_in(key, part):
    return jax.random.permutation(jax.random.fold_in(key, 11), D)[:R1].astype(jnp.int32)


def draw_rows_out(key, part):
    return jax.random.permutation(jax.random.fold_in(key, 23), D)[:R2].astype(jnp.int32)


def with_ends(values, own_key, low, top_value):
    longest = values.shape.index(max(values.shape))
    spots = []
    for shift in (0, 1):
        where = [jax.random.randint(jax.random.fold_in(own_key, axis), (), 0, length) for axis, length in enumerate(values.shape)]
        where[longest] = (where[longest] + shift) % values.shape[longest]
        spots.append(tuple(where))
    return values.at[spots[0]].set(low).at[spots[1]].set(top_value)


def steps_of(own_key, dims, pieces, smallest, largest):
    level = 1.0
    for dim, shards_of in pieces:
        heights = jax.random.uniform(jax.random.fold_in(jax.random.fold_in(own_key, 6), dim), (shards_of,), jnp.float32, smallest / len(pieces), largest / len(pieces))
        level = level * jnp.repeat(jnp.exp(heights), dims[dim] // shards_of).reshape((-1,) + (1,) * (len(dims) - 1 - dim))
    return level


def normal_values(own_key, shape, spread, limit, pieces=(), held_as=jnp.bfloat16):
    values = jax.random.normal(own_key, shape, jnp.float32) * spread
    if len(pieces) > 0:
        values = steps_of(own_key, shape, pieces, -0.22, 0.18) * values
    return jnp.clip(values, min=-limit, max=limit).astype(held_as)


def setup_inputs(seed: int = 0) -> dict:
    splits = jax.random.split(jax.random.key(seed), 11)
    return {
        "inputs": normal_values(splits[0], (EXAMPLES, TOK, D), 1.0, 6.0, ((0, 4), (1, 8))),
        "out_grads": normal_values(splits[1], (EXAMPLES, TOK, D), 0.0625, 0.5, ((0, 4), (2, 8))),
        "first_moment": normal_values(splits[2], (D, D), 0.3, 2.0, ((1, 8),), jnp.float32),
        "second_moment": jnp.clip(jnp.exp(math.log(1.0) - 4.6051702 * jax.random.uniform(splits[3], (D, D), jnp.float32) ** steps_of(splits[3], (D, D), ((1, 8),), -0.2, 0.2)), 0.01, 1.0),
        "signs_in": with_ends(jax.random.randint(splits[4], (D,), 0, 2), jax.random.fold_in(splits[4], 1), 0, 1).astype(jnp.int32),
        "signs_out": with_ends(jax.random.randint(splits[5], (D,), 0, 2), jax.random.fold_in(splits[5], 1), 0, 1).astype(jnp.int32),
        "rows_in": draw_rows_in(jax.random.fold_in(splits[10], 71), 0),
        "rows_out": draw_rows_out(jax.random.fold_in(splits[10], 71), 0),
        "task_ids": with_ends(jax.random.randint(splits[8], (EXAMPLES,), 0, NPROTO), jax.random.fold_in(splits[8], 1), 0, NPROTO - 1).astype(jnp.int32),
        "weights": with_ends(jax.random.randint(splits[9], (EXAMPLES,), 1, 5), jax.random.fold_in(splits[9], 1), 1, 4).astype(jnp.int32),
    }


def hadamard_rows(rows, sign_bits):
    cols = jnp.arange(D, dtype=jnp.int32)
    both = jnp.bitwise_and(rows[:, None], cols[None, :])
    parity = jnp.zeros(both.shape, jnp.int32)
    for bit in range(int(math.log2(D)) + 1):
        parity = jnp.bitwise_xor(parity, jnp.bitwise_and(jnp.right_shift(both, bit), 1))
    value = (1 - 2 * parity) * (1 - 2 * sign_bits)[None, :]
    return value.astype(jnp.float32)

def reference(inputs, out_grads, first_moment, second_moment, signs_in, signs_out, rows_in, rows_out, task_ids, weights):
    left = hadamard_rows(rows_in, signs_in).astype(jnp.bfloat16)
    right = hadamard_rows(rows_out, signs_out)
    protos = jnp.arange(NPROTO, dtype=jnp.int32)

    def one(total, idx):
        grad = jnp.dot(inputs[idx].T, out_grads[idx], preferred_element_type=jnp.float32)
        first = 0.9 * first_moment + 0.1 * grad
        second = 0.999 * second_moment + 0.001 * grad * grad
        update = (first / (jnp.sqrt(second) + 1e-08)).astype(jnp.bfloat16)
        half = jnp.dot(left, update, preferred_element_type=jnp.float32)
        sketch = jnp.dot(half, right.T, precision=lax.Precision.HIGHEST)
        unit = sketch * lax.rsqrt(jnp.mean(sketch * sketch) + 1e-06)
        coef = jnp.where(protos == task_ids[idx], weights[idx].astype(jnp.float32), jnp.float32(0.0))
        return (total + coef[:, None, None] * unit[None], None)
    start = jnp.zeros((NPROTO, R1, R2), jnp.float32)
    total, _ = lax.scan(one, start, jnp.arange(EXAMPLES, dtype=jnp.int32))
    return total
```

```python
import functools

import jax
import jax.numpy as jnp
from jax import lax
from jax.experimental import pallas as pl
from jax.experimental.pallas import tpu as pltpu
from jax.sharding import PartitionSpec as P

PRO_GRP = 2
CORES = 2
BLOCK = 512
TILE = 256


def signed_hadamard(rows, cols, sign_bits):
    parity = lax.population_count(jnp.bitwise_and(rows, cols)) + sign_bits
    return (1 - 2 * jnp.bitwise_and(parity, 1)).astype(jnp.bfloat16)


def sketch_kernel(n_parts, *refs):
    parts = refs[:n_parts]
    og_ref, first_ref, second_ref, left_ref, right_ref, out_ref = refs[n_parts : n_parts + 6]
    first_s, second_s, xt_0, xt_1, g_0, g_1, u_0, u_1, t_0, t_1 = refs[n_parts + 6 :]
    xt_s, g_s, u_s, t_s = (xt_0, xt_1), (g_0, g_1), (u_0, u_1), (t_0, t_1)
    examples, _, cols = og_ref.shape
    n_right = right_ref.shape[1]
    tile = g_0.shape[1]

    @pl.when(pl.program_id(0) == 0)
    def _():
        out_ref[...] = jnp.zeros_like(out_ref)

    first_s[...] = 9.0 * first_ref[...]
    second_s[...] = 99.9 * second_ref[...]
    items = [(e, c) for e in range(examples) for c in range(0, cols, tile)]

    def load(e):
        pieces = []
        for part in parts:
            if len(part.shape) == 4:
                pieces += [part[j, e] for j in range(part.shape[0])]
            else:
                pieces.append(part[e])
        x = jnp.concatenate(pieces, axis=0) if len(pieces) > 1 else pieces[0]
        xt_s[e % 2][...] = x.T

    def make_grad(i):
        e, c = items[i]
        if c == 0:
            load(e)
        g_s[i % 2][...] = jnp.dot(
            xt_s[e % 2][...], og_ref[e, :, c : c + tile], preferred_element_type=jnp.float32
        )

    def make_update(i):
        e, c = items[i]
        g = g_s[i % 2][...]
        first = first_s[:, c : c + tile] + g
        second = second_s[:, c : c + tile] + (0.1 * g) * g
        bottom = second * lax.rsqrt(second) + 1e-07
        u_s[e % 2][:, c : c + tile] = (first * pl.reciprocal(bottom, approx=True)).astype(
            jnp.bfloat16
        )

    def times_right(i):
        e, c = items[i]
        t = jnp.dot(
            u_s[e % 2][:, c : c + tile],
            right_ref[c : c + tile, :],
            preferred_element_type=jnp.float32,
        )
        if c == 0:
            t_s[e % 2][...] = t
        else:
            t_s[e % 2][...] += t

    def times_left(i):
        e, c = items[i]
        if c + tile != cols:
            return
        t = t_s[e % 2][...]
        high = t.astype(jnp.bfloat16)
        low = (t - high.astype(jnp.float32)).astype(jnp.bfloat16)
        both = jnp.dot(
            left_ref[...],
            jnp.concatenate([high, low], axis=1),
            preferred_element_type=jnp.float32,
        )
        out_ref[e] += both[:, :n_right] + both[:, n_right:]

    stages = (make_grad, make_update, times_right, times_left)
    for step in range(len(items) + len(stages) - 1):
        for lag, stage in enumerate(stages):
            if 0 <= step - lag < len(items):
                stage(step - lag)


def chunk_sketch(parts, starts, out_grads, first, second, left, right, start, rows):
    examples, tokens, cols = out_grads.shape
    n_left, n_right = left.shape[0], right.shape[1]
    block = min(BLOCK, rows)
    tile = min(TILE, cols)
    at = start // block

    def part_spec(part, part_start):
        off = part_start // block
        if part.ndim == 4:
            return pl.BlockSpec(part.shape[:3] + (block,), lambda i: (0, 0, 0, i + off))
        return pl.BlockSpec(part.shape[:2] + (block,), lambda i: (0, 0, i + off))

    elements = examples * rows * cols
    return pl.pallas_call(
        functools.partial(sketch_kernel, len(parts)),
        grid=(rows // block,),
        in_specs=[part_spec(part, s) for part, s in zip(parts, starts)]
        + [
            pl.BlockSpec((examples, tokens, cols), lambda i: (0, 0, 0)),
            pl.BlockSpec((block, cols), lambda i: (i + at, 0)),
            pl.BlockSpec((block, cols), lambda i: (i + at, 0)),
            pl.BlockSpec((n_left, block), lambda i: (0, i + at)),
            pl.BlockSpec((cols, n_right), lambda i: (0, 0)),
        ],
        out_specs=pl.BlockSpec((examples, n_left, n_right), lambda i: (0, 0, 0)),
        out_shape=jax.ShapeDtypeStruct((examples, n_left, n_right), jnp.float32),
        scratch_shapes=[pltpu.VMEM((block, cols), jnp.float32)] * 2
        + [pltpu.VMEM((block, tokens), jnp.bfloat16)] * 2
        + [pltpu.VMEM((block, tile), jnp.float32)] * 2
        + [pltpu.VMEM((block, cols), jnp.bfloat16)] * 2
        + [pltpu.VMEM((block, n_right), jnp.float32)] * 2,
        compiler_params=pltpu.CompilerParams(
            vmem_limit_bytes=48 * 1024 * 1024, dimension_semantics=("arbitrary",)
        ),
        cost_estimate=pl.CostEstimate(
            flops=2 * elements * (tokens + n_right),
            bytes_accessed=2 * rows * cols * 4,
            transcendentals=2 * elements,
        ),
        name="chunk_sketch",
    )(*parts, out_grads, first, second, left, right)


def hop(value, n_col, way, first_chip):
    chips = n_col // CORES
    pairs = []
    for z in range(first_chip, chips - 1):
        a, b = (z, z + 1) if way > 0 else (chips - 1 - z, chips - 2 - z)
        pairs += [(a * CORES + c, b * CORES + c) for c in range(CORES)]
    return lax.ppermute(value, "col", pairs)


def pair_sum(value, axis, size):
    bit = 1
    while bit < size:
        value = value + lax.ppermute(value, axis, [(i, i ^ bit) for i in range(size)])
        bit *= 2
    return value


def line_sketch(inputs, out_grads, first, second, left, right, n_col, chunks):
    chips = n_col // CORES
    me = lax.axis_index("col")
    z, core = me // CORES, me % CORES
    swap = [(i, i ^ 1) for i in range(n_col)]
    share = inputs.shape[1]
    blocks = [
        lax.rem(z - j + chips, chips) * CORES + c for c in (core, 1 - core) for j in range(chips)
    ]
    og = jnp.concatenate(
        [lax.dynamic_slice_in_dim(out_grads, b * share, share, 1) for b in blocks], axis=1
    )
    sibling = lax.ppermute(inputs, "col", swap)
    total = None
    start = 0
    for rows in chunks:
        piece = inputs[:, :, start : start + rows]
        ups, downs = [piece], [piece]
        for d in range(chips - 1):
            ups.append(hop(ups[-1], n_col, 1, d))
            downs.append(hop(downs[-1], n_col, -1, d))
        others = jnp.stack(
            [jnp.where(z >= j, ups[j], downs[chips - j]) for j in range(1, chips)]
        )
        others_sibling = lax.ppermute(others, "col", swap)
        part = chunk_sketch(
            [inputs, others, sibling, others_sibling],
            [start, 0, start, 0],
            og, first, second, left, right, start, rows,
        )
        total = part if total is None else total + part
        start += rows
    return total


def body(
    inputs,
    out_grads,
    first_moment,
    second_moment,
    signs_in,
    signs_out,
    rows_in,
    rows_out,
    task_ids,
    weights,
):
    width, local_cols = first_moment.shape
    n_col = lax.axis_size("col")
    n_grp = lax.axis_size("grp")
    me_col = lax.axis_index("col")
    left = signed_hadamard(
        rows_in[:, None], jnp.arange(width, dtype=jnp.int32)[None, :], signs_in[None, :]
    )
    offset = me_col * local_cols
    mine = offset + jnp.arange(local_cols, dtype=jnp.int32)
    signs_mine = lax.dynamic_slice_in_dim(signs_out, offset, local_cols, 0)
    right = signed_hadamard(rows_out[None, :], mine[:, None], signs_mine[:, None])
    if inputs.shape[1] % 16 == 0:
        chunks = [width // 8] * 8
        part = line_sketch(
            inputs, out_grads, first_moment, second_moment, left, right, n_col, chunks
        )
    else:
        whole = lax.all_gather(inputs, "col", axis=1, tiled=True)
        part = chunk_sketch(
            [whole], [0], out_grads, first_moment, second_moment, left, right, 0, width
        )
    sketch = pair_sum(part, "col", n_col)
    squares = jnp.sum(sketch * sketch, axis=(1, 2))
    entries = sketch.shape[1] * sketch.shape[2]
    owned = sketch.shape[1] // n_col
    unit = lax.dynamic_slice_in_dim(sketch, me_col * owned, owned, 1)
    unit = unit * lax.rsqrt(squares / entries + 1e-06)[:, None, None]
    protos = jnp.arange(PRO_GRP * n_grp, dtype=jnp.int32)
    coef = jnp.where(
        task_ids[:, None] == protos[None, :], weights[:, None].astype(jnp.float32), 0.0
    )
    term = jnp.sum(coef[:, :, None, None] * unit[:, None], axis=0)
    term = pair_sum(term, "grp", n_grp)
    return lax.dynamic_slice_in_dim(term, lax.axis_index("grp") * PRO_GRP, PRO_GRP, 0)


def solution(mesh):
    placed = (
        P("grp", "col", None),
        P("grp", None, "col"),
        P(None, "col"),
        P(None, "col"),
        P(),
        P(),
        P(),
        P(),
        P("grp"),
        P("grp"),
    )
    return jax.shard_map(
        body, mesh=mesh, in_specs=placed, out_specs=P("grp", "col", None), check_vma=False
    )
```

```python
import jax
import jax.numpy as jnp
from jax import lax
from jax.experimental import pallas as pl
from jax.experimental.pallas import tpu as pltpu
from jax.sharding import PartitionSpec as P

PRO_GRP = 2
BLOCK = 512
TILE = 256


def signed_hadamard(rows, cols, sign_bits):
    parity = lax.population_count(jnp.bitwise_and(rows, cols)) + sign_bits
    return (1 - 2 * jnp.bitwise_and(parity, 1)).astype(jnp.bfloat16)


def sketch_kernel(
    x_ref, og_ref, first_ref, second_ref, left_ref, right_ref, out_ref,
    first_s, second_s, xt_0, xt_1, g_0, g_1, u_0, u_1, t_0, t_1,
):
    xt_s, g_s, u_s, t_s = (xt_0, xt_1), (g_0, g_1), (u_0, u_1), (t_0, t_1)
    examples, _, cols = og_ref.shape
    n_right = right_ref.shape[1]
    tile = g_0.shape[1]

    @pl.when(pl.program_id(0) == 0)
    def _():
        out_ref[...] = jnp.zeros_like(out_ref)

    first_s[...] = 9.0 * first_ref[...]
    second_s[...] = 99.9 * second_ref[...]
    items = [(e, c) for e in range(examples) for c in range(0, cols, tile)]

    def make_grad(i):
        e, c = items[i]
        if c == 0:
            xt_s[e % 2][...] = x_ref[e].T
        g_s[i % 2][...] = jnp.dot(
            xt_s[e % 2][...], og_ref[e, :, c : c + tile], preferred_element_type=jnp.float32
        )

    def make_update(i):
        e, c = items[i]
        g = g_s[i % 2][...]
        first = first_s[:, c : c + tile] + g
        second = second_s[:, c : c + tile] + (0.1 * g) * g
        bottom = second * lax.rsqrt(second) + 1e-07
        u_s[e % 2][:, c : c + tile] = (first * pl.reciprocal(bottom, approx=True)).astype(
            jnp.bfloat16
        )

    def times_right(i):
        e, c = items[i]
        t = jnp.dot(
            u_s[e % 2][:, c : c + tile],
            right_ref[c : c + tile, :],
            preferred_element_type=jnp.float32,
        )
        if c == 0:
            t_s[e % 2][...] = t
        else:
            t_s[e % 2][...] += t

    def times_left(i):
        e, c = items[i]
        if c + tile != cols:
            return
        t = t_s[e % 2][...]
        high = t.astype(jnp.bfloat16)
        low = (t - high.astype(jnp.float32)).astype(jnp.bfloat16)
        both = jnp.dot(
            left_ref[...],
            jnp.concatenate([high, low], axis=1),
            preferred_element_type=jnp.float32,
        )
        out_ref[e] += both[:, :n_right] + both[:, n_right:]

    stages = (make_grad, make_update, times_right, times_left)
    for step in range(len(items) + len(stages) - 1):
        for lag, stage in enumerate(stages):
            if 0 <= step - lag < len(items):
                stage(step - lag)


def piece_sketch(gathered, out_grads, first, second, left, right, first_example, start):
    examples, tokens, rows = gathered.shape
    cols = out_grads.shape[2]
    n_left, n_right = left.shape[0], right.shape[1]
    block = min(BLOCK, rows)
    tile = min(TILE, cols)
    at = start // block
    group = first_example // examples
    elements = examples * rows * cols
    return pl.pallas_call(
        sketch_kernel,
        grid=(rows // block,),
        in_specs=[
            pl.BlockSpec((examples, tokens, block), lambda i: (0, 0, i)),
            pl.BlockSpec((examples, tokens, cols), lambda i: (group, 0, 0)),
            pl.BlockSpec((block, cols), lambda i: (i + at, 0)),
            pl.BlockSpec((block, cols), lambda i: (i + at, 0)),
            pl.BlockSpec((n_left, block), lambda i: (0, i + at)),
            pl.BlockSpec((cols, n_right), lambda i: (0, 0)),
        ],
        out_specs=pl.BlockSpec((examples, n_left, n_right), lambda i: (0, 0, 0)),
        out_shape=jax.ShapeDtypeStruct((examples, n_left, n_right), jnp.float32),
        scratch_shapes=[pltpu.VMEM((block, cols), jnp.float32)] * 2
        + [pltpu.VMEM((block, tokens), jnp.bfloat16)] * 2
        + [pltpu.VMEM((block, tile), jnp.float32)] * 2
        + [pltpu.VMEM((block, cols), jnp.bfloat16)] * 2
        + [pltpu.VMEM((block, n_right), jnp.float32)] * 2,
        compiler_params=pltpu.CompilerParams(
            vmem_limit_bytes=48 * 1024 * 1024, dimension_semantics=("arbitrary",)
        ),
        cost_estimate=pl.CostEstimate(
            flops=2 * elements * (tokens + n_right),
            bytes_accessed=2 * rows * cols * 4,
            transcendentals=2 * elements,
        ),
        name="piece_sketch",
    )(gathered, out_grads, first, second, left, right)


def pair_sum(value, axis, size):
    bit = 1
    while bit < size:
        value = value + lax.ppermute(value, axis, [(i, i ^ bit) for i in range(size)])
        bit *= 2
    return value


def body(
    inputs,
    out_grads,
    first_moment,
    second_moment,
    signs_in,
    signs_out,
    rows_in,
    rows_out,
    task_ids,
    weights,
):
    width, local_cols = first_moment.shape
    n_col = lax.axis_size("col")
    n_grp = lax.axis_size("grp")
    me_col = lax.axis_index("col")
    left = signed_hadamard(
        rows_in[:, None], jnp.arange(width, dtype=jnp.int32)[None, :], signs_in[None, :]
    )
    offset = me_col * local_cols
    mine = offset + jnp.arange(local_cols, dtype=jnp.int32)
    signs_mine = lax.dynamic_slice_in_dim(signs_out, offset, local_cols, 0)
    right = signed_hadamard(rows_out[None, :], mine[:, None], signs_mine[:, None])
    examples = inputs.shape[0]
    early = examples * 2 // 3
    most = width * 3 // 4
    pieces = [
        (0, early, 0, width),
        (early, examples - early, 0, most),
        (early, examples - early, most, width - most),
    ]
    sources = [inputs[e : e + n, :, r : r + rows] for e, n, r, rows in pieces]
    left, sources[1] = lax.optimization_barrier((left, sources[1]))
    gathered, parts = [], []
    for i, (e, n, r, rows) in enumerate(pieces):
        if i >= 2:
            gathered[i - 2], sources[i] = lax.optimization_barrier((gathered[i - 2], sources[i]))
        gathered.append(lax.all_gather(sources[i], "col", axis=1, tiled=True))
    for i, (e, n, r, rows) in enumerate(pieces):
        if i >= 1:
            parts[i - 1], gathered[i] = lax.optimization_barrier((parts[i - 1], gathered[i]))
        if i == 2:
            sketch, gathered[i] = lax.optimization_barrier((sketch, gathered[i]))
        parts.append(
            piece_sketch(gathered[i], out_grads, first_moment, second_moment, left, right, e, r)
        )
        if i == 1:
            sketch = pair_sum(parts[0], "col", n_col)
    sketch = jnp.concatenate([sketch, pair_sum(parts[1] + parts[2], "col", n_col)])
    squares = jnp.sum(sketch * sketch, axis=(1, 2))
    entries = sketch.shape[1] * sketch.shape[2]
    owned = sketch.shape[1] // n_col
    unit = lax.dynamic_slice_in_dim(sketch, me_col * owned, owned, 1)
    unit = unit * lax.rsqrt(squares / entries + 1e-06)[:, None, None]
    protos = jnp.arange(PRO_GRP * n_grp, dtype=jnp.int32)
    coef = jnp.where(
        task_ids[:, None] == protos[None, :], weights[:, None].astype(jnp.float32), 0.0
    )
    term = jnp.sum(coef[:, :, None, None] * unit[:, None], axis=0)
    term = pair_sum(term, "grp", n_grp)
    return lax.dynamic_slice_in_dim(term, lax.axis_index("grp") * PRO_GRP, PRO_GRP, 0)


def solution(mesh):
    placed = (
        P("grp", "col", None),
        P("grp", None, "col"),
        P(None, "col"),
        P(None, "col"),
        P(),
        P(),
        P(),
        P(),
        P("grp"),
        P("grp"),
    )
    return jax.shard_map(
        body, mesh=mesh, in_specs=placed, out_specs=P("grp", "col", None), check_vma=False
    )
```

```python
import jax
import jax.numpy as jnp
from jax import lax
from jax.experimental import pallas as pl
from jax.experimental.pallas import tpu as pltpu
from jax.sharding import PartitionSpec as P

PRO_GRP = 2
BLOCK = 512
TILE = 256


def signed_hadamard(rows, cols, sign_bits):
    parity = lax.population_count(jnp.bitwise_and(rows, cols)) + sign_bits
    return (1 - 2 * jnp.bitwise_and(parity, 1)).astype(jnp.bfloat16)


def sketch_kernel(
    x_ref, og_ref, first_ref, second_ref, left_ref, right_ref, out_ref,
    first_s, second_s, xt_0, xt_1, g_0, g_1, u_0, u_1, t_0, t_1,
):
    xt_s, g_s, u_s, t_s = (xt_0, xt_1), (g_0, g_1), (u_0, u_1), (t_0, t_1)
    examples, _, cols = og_ref.shape
    n_right = right_ref.shape[1]
    tile = g_0.shape[1]

    @pl.when(pl.program_id(0) == 0)
    def _():
        out_ref[...] = jnp.zeros_like(out_ref)

    first_s[...] = 9.0 * first_ref[...]
    second_s[...] = 99.9 * second_ref[...]
    items = [(e, c) for e in range(examples) for c in range(0, cols, tile)]

    def make_grad(i):
        e, c = items[i]
        if c == 0:
            xt_s[e % 2][...] = x_ref[e].T
        g_s[i % 2][...] = jnp.dot(
            xt_s[e % 2][...], og_ref[e, :, c : c + tile], preferred_element_type=jnp.float32
        )

    def make_update(i):
        e, c = items[i]
        g = g_s[i % 2][...]
        first = first_s[:, c : c + tile] + g
        second = second_s[:, c : c + tile] + (0.1 * g) * g
        bottom = second * lax.rsqrt(second) + 1e-07
        u_s[e % 2][:, c : c + tile] = (first * pl.reciprocal(bottom, approx=True)).astype(
            jnp.bfloat16
        )

    def times_right(i):
        e, c = items[i]
        t = jnp.dot(
            u_s[e % 2][:, c : c + tile],
            right_ref[c : c + tile, :],
            preferred_element_type=jnp.float32,
        )
        if c == 0:
            t_s[e % 2][...] = t
        else:
            t_s[e % 2][...] += t

    def times_left(i):
        e, c = items[i]
        if c + tile != cols:
            return
        t = t_s[e % 2][...]
        high = t.astype(jnp.bfloat16)
        low = (t - high.astype(jnp.float32)).astype(jnp.bfloat16)
        both = jnp.dot(
            left_ref[...],
            jnp.concatenate([high, low], axis=1),
            preferred_element_type=jnp.float32,
        )
        out_ref[e] += both[:, :n_right] + both[:, n_right:]

    stages = (make_grad, make_update, times_right, times_left)
    for step in range(len(items) + len(stages) - 1):
        for lag, stage in enumerate(stages):
            if 0 <= step - lag < len(items):
                stage(step - lag)


def piece_sketch(gathered, out_grads, first, second, left, right, first_example, start):
    examples, tokens, rows = gathered.shape
    cols = out_grads.shape[2]
    n_left, n_right = left.shape[0], right.shape[1]
    block = min(BLOCK, rows)
    tile = min(TILE, cols)
    at = start // block
    group = first_example // examples
    elements = examples * rows * cols
    return pl.pallas_call(
        sketch_kernel,
        grid=(rows // block,),
        in_specs=[
            pl.BlockSpec((examples, tokens, block), lambda i: (0, 0, i)),
            pl.BlockSpec((examples, tokens, cols), lambda i: (group, 0, 0)),
            pl.BlockSpec((block, cols), lambda i: (i + at, 0)),
            pl.BlockSpec((block, cols), lambda i: (i + at, 0)),
            pl.BlockSpec((n_left, block), lambda i: (0, i + at)),
            pl.BlockSpec((cols, n_right), lambda i: (0, 0)),
        ],
        out_specs=pl.BlockSpec((examples, n_left, n_right), lambda i: (0, 0, 0)),
        out_shape=jax.ShapeDtypeStruct((examples, n_left, n_right), jnp.float32),
        scratch_shapes=[pltpu.VMEM((block, cols), jnp.float32)] * 2
        + [pltpu.VMEM((block, tokens), jnp.bfloat16)] * 2
        + [pltpu.VMEM((block, tile), jnp.float32)] * 2
        + [pltpu.VMEM((block, cols), jnp.bfloat16)] * 2
        + [pltpu.VMEM((block, n_right), jnp.float32)] * 2,
        compiler_params=pltpu.CompilerParams(
            vmem_limit_bytes=48 * 1024 * 1024, dimension_semantics=("arbitrary",)
        ),
        cost_estimate=pl.CostEstimate(
            flops=2 * elements * (tokens + n_right),
            bytes_accessed=2 * rows * cols * 4,
            transcendentals=2 * elements,
        ),
        name="piece_sketch",
    )(gathered, out_grads, first, second, left, right)


def pair_sum(value, axis, size, bit=1):
    while bit < size:
        value = value + lax.ppermute(value, axis, [(i, i ^ bit) for i in range(size)])
        bit *= 2
    return value


def body(
    inputs,
    out_grads,
    first_moment,
    second_moment,
    signs_in,
    signs_out,
    rows_in,
    rows_out,
    task_ids,
    weights,
):
    width, local_cols = first_moment.shape
    n_col = lax.axis_size("col")
    n_grp = lax.axis_size("grp")
    me_col = lax.axis_index("col")
    left = signed_hadamard(
        rows_in[:, None], jnp.arange(width, dtype=jnp.int32)[None, :], signs_in[None, :]
    )
    offset = me_col * local_cols
    mine = offset + jnp.arange(local_cols, dtype=jnp.int32)
    signs_mine = lax.dynamic_slice_in_dim(signs_out, offset, local_cols, 0)
    right = signed_hadamard(rows_out[None, :], mine[:, None], signs_mine[:, None])
    pieces = [(0, width // 2), (width // 2, 3 * width // 8), (7 * width // 8, width // 8)]
    sources = [inputs[:, :, r : r + rows] for r, rows in pieces]
    left, sources[1] = lax.optimization_barrier((left, sources[1]))
    gathered, parts = [], []
    for i in range(len(pieces)):
        if i >= 2:
            gathered[i - 2], sources[i] = lax.optimization_barrier((gathered[i - 2], sources[i]))
        gathered.append(lax.all_gather(sources[i], "col", axis=1, tiled=True))
    for i, (r, rows) in enumerate(pieces):
        if i >= 1:
            parts[i - 1], gathered[i] = lax.optimization_barrier((parts[i - 1], gathered[i]))
        parts.append(
            piece_sketch(gathered[i], out_grads, first_moment, second_moment, left, right, 0, r)
        )
    sketch = sum(parts)
    examples, n_left, n_right = sketch.shape
    owned = n_left // n_col
    sketch = sketch + lax.ppermute(sketch, "col", [(i, i ^ 1) for i in range(n_col)])
    sketch = sketch.reshape(examples, n_col // 2, 2, owned, n_right)
    sketch = lax.dynamic_index_in_dim(sketch, me_col % 2, 2, keepdims=False)
    sketch = pair_sum(sketch, "col", n_col, 2)
    squares = jnp.sum(sketch * sketch, axis=(1, 2, 3))
    squares = squares + lax.ppermute(squares, "col", [(i, i ^ 1) for i in range(n_col)])
    unit = lax.dynamic_index_in_dim(sketch, me_col // 2, 1, keepdims=False)
    unit = unit * lax.rsqrt(squares / (n_left * n_right) + 1e-06)[:, None, None]
    protos = jnp.arange(PRO_GRP * n_grp, dtype=jnp.int32)
    coef = jnp.where(
        task_ids[:, None] == protos[None, :], weights[:, None].astype(jnp.float32), 0.0
    )
    term = jnp.sum(coef[:, :, None, None] * unit[:, None], axis=0)
    term = pair_sum(term, "grp", n_grp)
    return lax.dynamic_slice_in_dim(term, lax.axis_index("grp") * PRO_GRP, PRO_GRP, 0)


def solution(mesh):
    placed = (
        P("grp", "col", None),
        P("grp", None, "col"),
        P(None, "col"),
        P(None, "col"),
        P(),
        P(),
        P(),
        P(),
        P("grp"),
        P("grp"),
    )
    return jax.shard_map(
        body, mesh=mesh, in_specs=placed, out_specs=P("grp", "col", None), check_vma=False
    )
```

```python
import functools

import jax
import jax.numpy as jnp
from jax import lax
from jax.experimental import pallas as pl
from jax.experimental.pallas import tpu as pltpu
from jax.sharding import PartitionSpec as P

PRO_GRP = 2
CORES = 2
BLOCK = 512
TILE = 256


def signed_hadamard(rows, cols, sign_bits):
    parity = lax.population_count(jnp.bitwise_and(rows, cols)) + sign_bits
    return (1 - 2 * jnp.bitwise_and(parity, 1)).astype(jnp.bfloat16)


def sketch_kernel(n_parts, slots_ref, *refs):
    parts = refs[:n_parts]
    og_ref, first_ref, second_ref, left_ref, right_ref, out_ref = refs[n_parts : n_parts + 6]
    first_s, second_s, x_s, xt_0, xt_1, g_0, g_1, u_0, u_1, t_0, t_1 = refs[n_parts + 6 :]
    xt_s, g_s, u_s, t_s = (xt_0, xt_1), (g_0, g_1), (u_0, u_1), (t_0, t_1)
    examples, _, cols = og_ref.shape
    n_right = right_ref.shape[1]
    tile = g_0.shape[1]

    @pl.when(pl.program_id(0) == 0)
    def _():
        out_ref[...] = jnp.zeros_like(out_ref)

    first_s[...] = 9.0 * first_ref[...]
    second_s[...] = 99.9 * second_ref[...]
    items = [(e, c) for e in range(examples) for c in range(0, cols, tile)]

    def load(e):
        if n_parts == 1:
            xt_s[e % 2][...] = parts[0][e].T
            return
        slot = 0
        for part in parts:
            pieces = [part] if len(part.shape) == 3 else [part.at[j] for j in range(part.shape[0])]
            for piece in pieces:
                share = piece.shape[1]
                token = pl.multiple_of(slots_ref[slot] * share, share)
                x_s[pl.ds(token, share), :] = piece[e]
                slot += 1
        xt_s[e % 2][...] = x_s[: og_ref.shape[1], :].T

    def make_grad(i):
        e, c = items[i]
        if c == 0:
            load(e)
        g_s[i % 2][...] = jnp.dot(
            xt_s[e % 2][...], og_ref[e, :, c : c + tile], preferred_element_type=jnp.float32
        )

    def make_update(i):
        e, c = items[i]
        g = g_s[i % 2][...]
        first = first_s[:, c : c + tile] + g
        second = second_s[:, c : c + tile] + (0.1 * g) * g
        bottom = second * lax.rsqrt(second) + 1e-07
        u_s[e % 2][:, c : c + tile] = (first * pl.reciprocal(bottom, approx=True)).astype(
            jnp.bfloat16
        )

    def times_right(i):
        e, c = items[i]
        t = jnp.dot(
            u_s[e % 2][:, c : c + tile],
            right_ref[c : c + tile, :],
            preferred_element_type=jnp.float32,
        )
        if c == 0:
            t_s[e % 2][...] = t
        else:
            t_s[e % 2][...] += t

    def times_left(i):
        e, c = items[i]
        if c + tile != cols:
            return
        t = t_s[e % 2][...]
        high = t.astype(jnp.bfloat16)
        low = (t - high.astype(jnp.float32)).astype(jnp.bfloat16)
        both = jnp.dot(
            left_ref[...],
            jnp.concatenate([high, low], axis=1),
            preferred_element_type=jnp.float32,
        )
        out_ref[e] += both[:, :n_right] + both[:, n_right:]

    stages = (make_grad, make_update, times_right, times_left)
    for step in range(len(items) + len(stages) - 1):
        for lag, stage in enumerate(stages):
            if 0 <= step - lag < len(items):
                stage(step - lag)


def piece_sketch(slots, parts, starts, out_grads, first, second, left, right, start, rows):
    examples, tokens, cols = out_grads.shape
    n_left, n_right = left.shape[0], right.shape[1]
    block = min(BLOCK, rows)
    tile = min(TILE, cols)
    at = start // block

    def part_spec(part, part_start):
        off = part_start // block
        if part.ndim == 4:
            return pl.BlockSpec(part.shape[:3] + (block,), lambda i: (0, 0, 0, i + off))
        return pl.BlockSpec(part.shape[:2] + (block,), lambda i: (0, 0, i + off))

    return pl.pallas_call(
        functools.partial(sketch_kernel, len(parts)),
        grid=(rows // block,),
        in_specs=[pl.BlockSpec(memory_space=pltpu.SMEM)]
        + [part_spec(part, s) for part, s in zip(parts, starts)]
        + [
            pl.BlockSpec((examples, tokens, cols), lambda i: (0, 0, 0)),
            pl.BlockSpec((block, cols), lambda i: (i + at, 0)),
            pl.BlockSpec((block, cols), lambda i: (i + at, 0)),
            pl.BlockSpec((n_left, block), lambda i: (0, i + at)),
            pl.BlockSpec((cols, n_right), lambda i: (0, 0)),
        ],
        out_specs=pl.BlockSpec((examples, n_left, n_right), lambda i: (0, 0, 0)),
        out_shape=jax.ShapeDtypeStruct((examples, n_left, n_right), jnp.float32),
        scratch_shapes=[pltpu.VMEM((block, cols), jnp.float32)] * 2
        + [pltpu.VMEM((tokens + parts[0].shape[1], block), jnp.bfloat16)]
        + [pltpu.VMEM((block, tokens), jnp.bfloat16)] * 2
        + [pltpu.VMEM((block, tile), jnp.float32)] * 2
        + [pltpu.VMEM((block, cols), jnp.bfloat16)] * 2
        + [pltpu.VMEM((block, n_right), jnp.float32)] * 2,
        compiler_params=pltpu.CompilerParams(
            vmem_limit_bytes=48 * 1024 * 1024, dimension_semantics=("arbitrary",)
        ),
        cost_estimate=pl.CostEstimate(flops=1, bytes_accessed=1, transcendentals=0),
        name="piece_sketch",
    )(slots, *parts, out_grads, first, second, left, right)


def pair_sum(value, axis, size, bit=1):
    while bit < size:
        value = value + lax.ppermute(value, axis, [(i, i ^ bit) for i in range(size)])
        bit *= 2
    return value


def all_sketches(inputs, out_grads, first, second, left, right, hops, gathers):
    chips = lax.axis_size("col") // CORES
    me = lax.axis_index("col")
    z, core = me // CORES, me % CORES
    slots = [lax.rem(z - j + chips, chips) * CORES + c for c in (core, 1 - core) for j in range(chips)]
    slots = jnp.stack(slots).astype(jnp.int32)
    starts, rest = [], 0
    for rows in hops + gathers:
        starts.append(rest)
        rest += rows
    sources = [inputs[:, :, s : s + rows] for s, rows in zip(starts, hops + gathers)]
    n = len(hops)

    def hop(value, way, first_chip):
        pairs = []
        for a in range(first_chip, chips - 1):
            a, b = (a, a + 1) if way > 0 else (chips - 1 - a, chips - 2 - a)
            pairs += [(a * CORES + c, b * CORES + c) for c in range(CORES)]
        return lax.ppermute(value, "col", pairs)

    def swap(value):
        return lax.ppermute(value, "col", [(i, i ^ 1) for i in range(chips * CORES)])

    def sketch_of(k, parts, part_starts):
        return piece_sketch(
            slots, parts, part_starts, out_grads, first, second, left, right,
            starts[k], (hops + gathers)[k],
        )

    arrived, swapped = [], []
    if n > 0:
        sibling = swap(inputs)
    for k in range(n):
        ups, downs = [sources[k]], [sources[k]]
        for d in range(chips - 1):
            ups.append(hop(ups[-1], 1, d))
            downs.append(hop(downs[-1], -1, d))
        others = jnp.stack(
            [jnp.where(z >= j, ups[j], downs[chips - j]) for j in range(1, chips)]
        )
        if k == 0:
            others, *sources[n:] = lax.optimization_barrier((others, *sources[n:]))
        arrived.append(others)
        swapped.append(swap(others))
    if n > 0:
        *arrived, sources[n] = lax.optimization_barrier((*arrived, sources[n]))
    parts, gathered = [], []
    for k in range(n):
        mine, theirs = arrived[k], swapped[k]
        if k > 0:
            parts[-1], mine = lax.optimization_barrier((parts[-1], mine))
        parts.append(sketch_of(k, [inputs, mine, sibling, theirs], [starts[k], 0, starts[k], 0]))
    if n > 0:
        parts[0], sources[n + 1] = lax.optimization_barrier((parts[0], sources[n + 1]))
    else:
        left, sources[1] = lax.optimization_barrier((left, sources[1]))
    for k in range(n, len(sources)):
        if k >= max(2, n + 2):
            gathered[k - n - 2], sources[k] = lax.optimization_barrier(
                (gathered[k - n - 2], sources[k])
            )
        gathered.append(lax.all_gather(sources[k], "col", axis=1, tiled=True))
    for k, whole in zip(range(n, len(sources)), gathered):
        if parts:
            parts[-1], whole = lax.optimization_barrier((parts[-1], whole))
        parts.append(sketch_of(k, [whole], [0]))
    return parts


def body(
    inputs,
    out_grads,
    first_moment,
    second_moment,
    signs_in,
    signs_out,
    rows_in,
    rows_out,
    task_ids,
    weights,
):
    width, local_cols = first_moment.shape
    n_col = lax.axis_size("col")
    n_grp = lax.axis_size("grp")
    me_col = lax.axis_index("col")
    left = signed_hadamard(
        rows_in[:, None], jnp.arange(width, dtype=jnp.int32)[None, :], signs_in[None, :]
    )
    offset = me_col * local_cols
    mine = offset + jnp.arange(local_cols, dtype=jnp.int32)
    signs_mine = lax.dynamic_slice_in_dim(signs_out, offset, local_cols, 0)
    right = signed_hadamard(rows_out[None, :], mine[:, None], signs_mine[:, None])
    sixteenth = width // 16
    hops, gathers = [], [8 * sixteenth, 6 * sixteenth, 2 * sixteenth]
    if n_col == 4 * CORES and inputs.shape[1] % 16 == 0:
        hops, gathers = [2 * sixteenth] * 4, [6 * sixteenth, 2 * sixteenth]
    sketch = sum(
        all_sketches(inputs, out_grads, first_moment, second_moment, left, right, hops, gathers)
    )
    examples, n_left, n_right = sketch.shape
    owned = n_left // n_col
    sketch = sketch + lax.ppermute(sketch, "col", [(i, i ^ 1) for i in range(n_col)])
    sketch = sketch.reshape(examples, n_col // 2, 2, owned, n_right)
    sketch = lax.dynamic_index_in_dim(sketch, me_col % 2, 2, keepdims=False)
    sketch = pair_sum(sketch, "col", n_col, 2)
    squares = jnp.sum(sketch * sketch, axis=(1, 2, 3))
    squares = squares + lax.ppermute(squares, "col", [(i, i ^ 1) for i in range(n_col)])
    unit = lax.dynamic_index_in_dim(sketch, me_col // 2, 1, keepdims=False)
    unit = unit * lax.rsqrt(squares / (n_left * n_right) + 1e-06)[:, None, None]
    protos = jnp.arange(PRO_GRP * n_grp, dtype=jnp.int32)
    coef = jnp.where(
        task_ids[:, None] == protos[None, :], weights[:, None].astype(jnp.float32), 0.0
    )
    term = jnp.sum(coef[:, :, None, None] * unit[:, None], axis=0)
    term = pair_sum(term, "grp", n_grp)
    return lax.dynamic_slice_in_dim(term, lax.axis_index("grp") * PRO_GRP, PRO_GRP, 0)


def solution(mesh):
    placed = (
        P("grp", "col", None),
        P("grp", None, "col"),
        P(None, "col"),
        P(None, "col"),
        P(),
        P(),
        P(),
        P(),
        P("grp"),
        P("grp"),
    )
    return jax.shard_map(
        body, mesh=mesh, in_specs=placed, out_specs=P("grp", "col", None), check_vma=False
    )
```

```python
import functools

import jax
import jax.numpy as jnp
from jax import lax
from jax.experimental import pallas as pl
from jax.experimental.pallas import tpu as pltpu
from jax.sharding import PartitionSpec as P

PRO_GRP = 2
CORES = 2
BLOCK = 512
TILE = 256


def signed_hadamard(rows, cols, sign_bits):
    parity = lax.population_count(jnp.bitwise_and(rows, cols)) + sign_bits
    return (1 - 2 * jnp.bitwise_and(parity, 1)).astype(jnp.bfloat16)


def sketch_kernel(n_parts, per, slots_ref, *refs):
    parts = refs[:n_parts]
    og_ref, first_ref, second_ref, left_ref, right_ref, out_ref = refs[n_parts : n_parts + 6]
    first_s, second_s, x_s, xt_0, xt_1, g_0, g_1, u_0, u_1, t_0, t_1 = refs[n_parts + 6 :]
    xt_s, g_s, u_s, t_s = (xt_0, xt_1), (g_0, g_1), (u_0, u_1), (t_0, t_1)
    examples, _, cols = og_ref.shape
    n_right = right_ref.shape[1]
    tile = g_0.shape[1]

    @pl.when(pl.program_id(0) == 0)
    def _():
        out_ref[...] = jnp.zeros_like(out_ref)

    first_s[...] = 9.0 * first_ref[...]
    second_s[...] = 99.9 * second_ref[...]
    items = [(e, c) for e in range(examples) for c in range(0, cols, tile)]

    if n_parts > 1:
        own_ref, sibling_ref = parts[:2]
        n_chunks = (n_parts - 2) // 2
        share = own_ref.shape[1]
        others = parts[2].shape[0]

        def place(slot, value):
            token = pl.multiple_of(slots_ref[slot] * share, share)
            x_s[:, pl.ds(token, share), :] = value

        place(0, own_ref[...])
        place(others + 1, sibling_ref[...])
        for k in range(n_chunks):

            @pl.when(pl.program_id(0) // per == k)
            def _():
                for j in range(others):
                    place(1 + j, parts[2 + k][j])
                    place(others + 2 + j, parts[2 + n_chunks + k][j])

    def load(e):
        xt_s[e % 2][...] = (parts[0][e] if n_parts == 1 else x_s[e]).T

    def make_grad(i):
        e, c = items[i]
        if c == 0:
            load(e)
        g_s[i % 2][...] = jnp.dot(
            xt_s[e % 2][...], og_ref[e, :, c : c + tile], preferred_element_type=jnp.float32
        )

    def make_update(i):
        e, c = items[i]
        g = g_s[i % 2][...]
        first = first_s[:, c : c + tile] + g
        second = second_s[:, c : c + tile] + (0.1 * g) * g
        bottom = second * lax.rsqrt(second) + 1e-07
        u_s[e % 2][:, c : c + tile] = (first * pl.reciprocal(bottom, approx=True)).astype(
            jnp.bfloat16
        )

    def times_right(i):
        e, c = items[i]
        t = jnp.dot(
            u_s[e % 2][:, c : c + tile],
            right_ref[c : c + tile, :],
            preferred_element_type=jnp.float32,
        )
        if c == 0:
            t_s[e % 2][...] = t
        else:
            t_s[e % 2][...] += t

    def times_left(i):
        e, c = items[i]
        if c + tile != cols:
            return
        t = t_s[e % 2][...]
        high = t.astype(jnp.bfloat16)
        low = (t - high.astype(jnp.float32)).astype(jnp.bfloat16)
        both = jnp.dot(
            left_ref[...],
            jnp.concatenate([high, low], axis=1),
            preferred_element_type=jnp.float32,
        )
        out_ref[e] += both[:, :n_right] + both[:, n_right:]

    stages = (make_grad, make_update, times_right, times_left)
    for step in range(len(items) + len(stages) - 1):
        for lag, stage in enumerate(stages):
            if 0 <= step - lag < len(items):
                stage(step - lag)


def piece_sketch(slots, parts, out_grads, first, second, left, right, start, rows):
    examples, tokens, cols = out_grads.shape
    n_left, n_right = left.shape[0], right.shape[1]
    block = min(BLOCK, rows)
    tile = min(TILE, cols)
    at = start // block

    n_chunks = (len(parts) - 2) // 2
    per = rows // block // n_chunks if n_chunks > 0 else 1

    def part_spec(i, part):
        if part.ndim == 3:
            return pl.BlockSpec(part.shape[:2] + (block,), lambda i: (0, 0, i))
        first_block = (i - 2) % n_chunks * per
        return pl.BlockSpec(
            part.shape[:3] + (block,),
            lambda i: (0, 0, 0, jnp.clip(i - first_block, 0, per - 1)),
        )

    return pl.pallas_call(
        functools.partial(sketch_kernel, len(parts), per),
        grid=(rows // block,),
        in_specs=[pl.BlockSpec(memory_space=pltpu.SMEM)]
        + [part_spec(i, part) for i, part in enumerate(parts)]
        + [
            pl.BlockSpec((examples, tokens, cols), lambda i: (0, 0, 0)),
            pl.BlockSpec((block, cols), lambda i: (i + at, 0)),
            pl.BlockSpec((block, cols), lambda i: (i + at, 0)),
            pl.BlockSpec((n_left, block), lambda i: (0, i + at)),
            pl.BlockSpec((cols, n_right), lambda i: (0, 0)),
        ],
        out_specs=pl.BlockSpec((examples, n_left, n_right), lambda i: (0, 0, 0)),
        out_shape=jax.ShapeDtypeStruct((examples, n_left, n_right), jnp.float32),
        scratch_shapes=[pltpu.VMEM((block, cols), jnp.float32)] * 2
        + [pltpu.VMEM((examples, tokens, block) if n_chunks > 0 else (1, 16, 128), jnp.bfloat16)]
        + [pltpu.VMEM((block, tokens), jnp.bfloat16)] * 2
        + [pltpu.VMEM((block, tile), jnp.float32)] * 2
        + [pltpu.VMEM((block, cols), jnp.bfloat16)] * 2
        + [pltpu.VMEM((block, n_right), jnp.float32)] * 2,
        compiler_params=pltpu.CompilerParams(
            vmem_limit_bytes=48 * 1024 * 1024, dimension_semantics=("arbitrary",)
        ),
        cost_estimate=pl.CostEstimate(flops=1, bytes_accessed=1, transcendentals=0),
        name="piece_sketch",
    )(slots, *parts, out_grads, first, second, left, right)


def pair_sum(value, axis, size, bit=1):
    while bit < size:
        value = value + lax.ppermute(value, axis, [(i, i ^ bit) for i in range(size)])
        bit *= 2
    return value


def all_sketches(inputs, out_grads, first, second, left, right, hops, gathers):
    chips = lax.axis_size("col") // CORES
    me = lax.axis_index("col")
    z, core = me // CORES, me % CORES
    slots = [lax.rem(z - j + chips, chips) * CORES + c for c in (core, 1 - core) for j in range(chips)]
    slots = jnp.stack(slots).astype(jnp.int32)
    starts, rest = [], 0
    for rows in hops + gathers:
        starts.append(rest)
        rest += rows
    sources = [inputs[:, :, s : s + rows] for s, rows in zip(starts, hops + gathers)]
    n = len(hops)

    def hop(value, way, first_chip):
        pairs = []
        for a in range(first_chip, chips - 1):
            a, b = (a, a + 1) if way > 0 else (chips - 1 - a, chips - 2 - a)
            pairs += [(a * CORES + c, b * CORES + c) for c in range(CORES)]
        return lax.ppermute(value, "col", pairs)

    def swap(value):
        return lax.ppermute(value, "col", [(i, i ^ 1) for i in range(chips * CORES)])

    def sketch_of(start, rows, blocks):
        return piece_sketch(
            slots, blocks, out_grads, first, second, left, right, start, rows
        )

    arrived, swapped = [], []
    if n > 0:
        sibling = swap(inputs)
    for k in range(n):
        ups, downs = [sources[k]], [sources[k]]
        for d in range(chips - 1):
            ups.append(hop(ups[-1], 1, d))
            downs.append(hop(downs[-1], -1, d))
        others = jnp.stack(
            [jnp.where(z >= j, ups[j], downs[chips - j]) for j in range(1, chips)]
        )
        if k == 0:
            others, *sources[n:] = lax.optimization_barrier((others, *sources[n:]))
        arrived.append(others)
        swapped.append(swap(others))
    if n > 0:
        *arrived, sources[n] = lax.optimization_barrier((*arrived, sources[n]))
    parts, gathered = [], []
    if n > 0:
        parts.append(sketch_of(0, sum(hops), [inputs, sibling, *arrived, *swapped]))
    if n > 0:
        parts[0], sources[n + 1] = lax.optimization_barrier((parts[0], sources[n + 1]))
    else:
        left, sources[1] = lax.optimization_barrier((left, sources[1]))
    for k in range(n, len(sources)):
        if k >= max(2, n + 2):
            gathered[k - n - 2], sources[k] = lax.optimization_barrier(
                (gathered[k - n - 2], sources[k])
            )
        gathered.append(lax.all_gather(sources[k], "col", axis=1, tiled=True))
    for k, whole in zip(range(n, len(sources)), gathered):
        if parts:
            parts[-1], whole = lax.optimization_barrier((parts[-1], whole))
        parts.append(sketch_of(starts[k], gathers[k - n], [whole]))
    return parts


def body(
    inputs,
    out_grads,
    first_moment,
    second_moment,
    signs_in,
    signs_out,
    rows_in,
    rows_out,
    task_ids,
    weights,
):
    width, local_cols = first_moment.shape
    n_col = lax.axis_size("col")
    n_grp = lax.axis_size("grp")
    me_col = lax.axis_index("col")
    left = signed_hadamard(
        rows_in[:, None], jnp.arange(width, dtype=jnp.int32)[None, :], signs_in[None, :]
    )
    offset = me_col * local_cols
    mine = offset + jnp.arange(local_cols, dtype=jnp.int32)
    signs_mine = lax.dynamic_slice_in_dim(signs_out, offset, local_cols, 0)
    right = signed_hadamard(rows_out[None, :], mine[:, None], signs_mine[:, None])
    sixteenth = width // 16
    hops, gathers = [], [8 * sixteenth, 6 * sixteenth, 2 * sixteenth]
    if n_col == 4 * CORES and inputs.shape[1] % 16 == 0:
        hops, gathers = [2 * sixteenth] * 4, [6 * sixteenth, 2 * sixteenth]
    sketch = sum(
        all_sketches(inputs, out_grads, first_moment, second_moment, left, right, hops, gathers)
    )
    examples, n_left, n_right = sketch.shape
    owned = n_left // n_col
    sketch = sketch + lax.ppermute(sketch, "col", [(i, i ^ 1) for i in range(n_col)])
    sketch = sketch.reshape(examples, n_col // 2, 2, owned, n_right)
    sketch = lax.dynamic_index_in_dim(sketch, me_col % 2, 2, keepdims=False)
    sketch = pair_sum(sketch, "col", n_col, 2)
    squares = jnp.sum(sketch * sketch, axis=(1, 2, 3))
    squares = squares + lax.ppermute(squares, "col", [(i, i ^ 1) for i in range(n_col)])
    unit = lax.dynamic_index_in_dim(sketch, me_col // 2, 1, keepdims=False)
    unit = unit * lax.rsqrt(squares / (n_left * n_right) + 1e-06)[:, None, None]
    protos = jnp.arange(PRO_GRP * n_grp, dtype=jnp.int32)
    coef = jnp.where(
        task_ids[:, None] == protos[None, :], weights[:, None].astype(jnp.float32), 0.0
    )
    term = jnp.sum(coef[:, :, None, None] * unit[:, None], axis=0)
    term = pair_sum(term, "grp", n_grp)
    return lax.dynamic_slice_in_dim(term, lax.axis_index("grp") * PRO_GRP, PRO_GRP, 0)


def solution(mesh):
    placed = (
        P("grp", "col", None),
        P("grp", None, "col"),
        P(None, "col"),
        P(None, "col"),
        P(),
        P(),
        P(),
        P(),
        P("grp"),
        P("grp"),
    )
    return jax.shard_map(
        body, mesh=mesh, in_specs=placed, out_specs=P("grp", "col", None), check_vma=False
    )
```

```python
import functools

import jax
import jax.numpy as jnp
from jax import lax
from jax.experimental import pallas as pl
from jax.experimental.pallas import tpu as pltpu
from jax.sharding import PartitionSpec as P

PRO_GRP = 2
CORES = 2
BLOCK = 512
TILE = 256


def signed_hadamard(rows, cols, sign_bits):
    parity = lax.population_count(jnp.bitwise_and(rows, cols)) + sign_bits
    return (1 - 2 * jnp.bitwise_and(parity, 1)).astype(jnp.bfloat16)


def sketch_kernel(n_parts, per, slots_ref, *refs):
    parts = refs[:n_parts]
    og_ref, first_ref, second_ref, left_ref, right_ref, out_ref = refs[n_parts : n_parts + 6]
    first_s, second_s, x_s, xt_0, xt_1, g_0, g_1, u_0, u_1, t_0, t_1 = refs[n_parts + 6 :]
    xt_s, g_s, u_s, t_s = (xt_0, xt_1), (g_0, g_1), (u_0, u_1), (t_0, t_1)
    examples, _, cols = og_ref.shape
    n_right = right_ref.shape[1]
    tile = g_0.shape[1]

    @pl.when(pl.program_id(0) == 0)
    def _():
        out_ref[...] = jnp.zeros_like(out_ref)

    first_s[...] = 9.0 * first_ref[...]
    second_s[...] = 99.9 * second_ref[...]
    items = [(e, c) for e in range(examples) for c in range(0, cols, tile)]

    if n_parts > 1:
        own_ref, sibling_ref = parts[:2]
        n_chunks = (n_parts - 2) // 2
        share = own_ref.shape[1]
        others = parts[2].shape[0]

        def place(slot, value):
            token = pl.multiple_of(slots_ref[slot] * share, share)
            x_s[:, pl.ds(token, share), :] = value

        place(0, own_ref[...])
        place(others + 1, sibling_ref[...])
        for k in range(n_chunks):

            @pl.when(pl.program_id(0) // per == k)
            def _():
                for j in range(others):
                    place(1 + j, parts[2 + k][j])
                    place(others + 2 + j, parts[2 + n_chunks + k][j])

    def load(e):
        xt_s[e % 2][...] = (parts[0][e] if n_parts == 1 else x_s[e]).T

    def make_grad(i):
        e, c = items[i]
        if c == 0:
            load(e)
        g_s[i % 2][...] = jnp.dot(
            xt_s[e % 2][...], og_ref[e, :, c : c + tile], preferred_element_type=jnp.float32
        )

    def make_update(i):
        e, c = items[i]
        g = g_s[i % 2][...]
        first = first_s[:, c : c + tile] + g
        second = second_s[:, c : c + tile] + (0.1 * g) * g
        bottom = second * lax.rsqrt(second) + 1e-07
        u_s[e % 2][:, c : c + tile] = (first * pl.reciprocal(bottom, approx=True)).astype(
            jnp.bfloat16
        )

    def times_right(i):
        e, c = items[i]
        t = jnp.dot(
            u_s[e % 2][:, c : c + tile],
            right_ref[c : c + tile, :],
            preferred_element_type=jnp.float32,
        )
        if c == 0:
            t_s[e % 2][...] = t
        else:
            t_s[e % 2][...] += t

    def times_left(i):
        e, c = items[i]
        if c + tile != cols:
            return
        t = t_s[e % 2][...]
        high = t.astype(jnp.bfloat16)
        low = (t - high.astype(jnp.float32)).astype(jnp.bfloat16)
        both = jnp.dot(
            left_ref[...],
            jnp.concatenate([high, low], axis=1),
            preferred_element_type=jnp.float32,
        )
        out_ref[e] += both[:, :n_right] + both[:, n_right:]

    stages = (make_grad, make_update, times_right, times_left)
    for step in range(len(items) + len(stages) - 1):
        for lag, stage in enumerate(stages):
            if 0 <= step - lag < len(items):
                stage(step - lag)


def piece_sketch(slots, parts, out_grads, first, second, left, right, start, rows):
    examples, tokens, cols = out_grads.shape
    n_left, n_right = left.shape[0], right.shape[1]
    block = min(BLOCK, rows)
    tile = min(TILE, cols)
    at = start // block

    n_chunks = (len(parts) - 2) // 2
    per = rows // block // n_chunks if n_chunks > 0 else 1

    def part_spec(i, part):
        if part.ndim == 3:
            return pl.BlockSpec(part.shape[:2] + (block,), lambda i: (0, 0, i))
        first_block = (i - 2) % n_chunks * per
        return pl.BlockSpec(
            part.shape[:3] + (block,),
            lambda i: (0, 0, 0, jnp.clip(i - first_block, 0, per - 1)),
        )

    return pl.pallas_call(
        functools.partial(sketch_kernel, len(parts), per),
        grid=(rows // block,),
        in_specs=[pl.BlockSpec(memory_space=pltpu.SMEM)]
        + [part_spec(i, part) for i, part in enumerate(parts)]
        + [
            pl.BlockSpec((examples, tokens, cols), lambda i: (0, 0, 0)),
            pl.BlockSpec((block, cols), lambda i: (i + at, 0)),
            pl.BlockSpec((block, cols), lambda i: (i + at, 0)),
            pl.BlockSpec((n_left, block), lambda i: (0, i + at)),
            pl.BlockSpec((cols, n_right), lambda i: (0, 0)),
        ],
        out_specs=pl.BlockSpec((examples, n_left, n_right), lambda i: (0, 0, 0)),
        out_shape=jax.ShapeDtypeStruct((examples, n_left, n_right), jnp.float32),
        scratch_shapes=[pltpu.VMEM((block, cols), jnp.float32)] * 2
        + [pltpu.VMEM((examples, tokens, block) if n_chunks > 0 else (1, 16, 128), jnp.bfloat16)]
        + [pltpu.VMEM((block, tokens), jnp.bfloat16)] * 2
        + [pltpu.VMEM((block, tile), jnp.float32)] * 2
        + [pltpu.VMEM((block, cols), jnp.bfloat16)] * 2
        + [pltpu.VMEM((block, n_right), jnp.float32)] * 2,
        compiler_params=pltpu.CompilerParams(
            vmem_limit_bytes=(60 if rows <= 2 * block else 48) * 1024 * 1024, dimension_semantics=("arbitrary",)
        ),
        cost_estimate=pl.CostEstimate(flops=1, bytes_accessed=1, transcendentals=0),
        name="piece_sketch",
    )(slots, *parts, out_grads, first, second, left, right)


def pair_sum(value, axis, size, bit=1):
    while bit < size:
        value = value + lax.ppermute(value, axis, [(i, i ^ bit) for i in range(size)])
        bit *= 2
    return value


def all_sketches(inputs, out_grads, first, second, left, right, hops, gathers):
    chips = lax.axis_size("col") // CORES
    me = lax.axis_index("col")
    z, core = me // CORES, me % CORES
    slots = [lax.rem(z - j + chips, chips) * CORES + c for c in (core, 1 - core) for j in range(chips)]
    slots = jnp.stack(slots).astype(jnp.int32)
    starts, rest = [], 0
    for rows in hops + gathers:
        starts.append(rest)
        rest += rows
    sources = [inputs[:, :, s : s + rows] for s, rows in zip(starts, hops + gathers)]
    n = len(hops)

    def hop(value, way, first_chip):
        pairs = []
        for a in range(first_chip, chips - 1):
            a, b = (a, a + 1) if way > 0 else (chips - 1 - a, chips - 2 - a)
            pairs += [(a * CORES + c, b * CORES + c) for c in range(CORES)]
        return lax.ppermute(value, "col", pairs)

    def swap(value):
        return lax.ppermute(value, "col", [(i, i ^ 1) for i in range(chips * CORES)])

    def sketch_of(start, rows, blocks):
        return piece_sketch(
            slots, blocks, out_grads, first, second, left, right, start, rows
        )

    arrived, swapped = [], []
    if n > 0:
        sibling = swap(inputs)
    for k in range(n):
        ups, downs = [sources[k]], [sources[k]]
        for d in range(chips - 1):
            ups.append(hop(ups[-1], 1, d))
            downs.append(hop(downs[-1], -1, d))
        others = jnp.stack(
            [jnp.where(z >= j, ups[j], downs[chips - j]) for j in range(1, chips)]
        )
        if k == 0:
            others, *sources[n:] = lax.optimization_barrier((others, *sources[n:]))
        arrived.append(others)
        swapped.append(swap(others))
    if n > 0:
        *arrived, sources[n] = lax.optimization_barrier((*arrived, sources[n]))
    parts, gathered = [], []
    if n > 0:
        parts.append(sketch_of(0, sum(hops), [inputs, sibling, *arrived, *swapped]))
    if n > 0:
        parts[0], sources[n + 1] = lax.optimization_barrier((parts[0], sources[n + 1]))
    else:
        left, sources[1] = lax.optimization_barrier((left, sources[1]))
    for k in range(n, len(sources)):
        if k >= max(2, n + 2):
            gathered[k - n - 2], sources[k] = lax.optimization_barrier(
                (gathered[k - n - 2], sources[k])
            )
        gathered.append(lax.all_gather(sources[k], "col", axis=1, tiled=True))
    for k, whole in zip(range(n, len(sources)), gathered):
        if parts:
            parts[-1], whole = lax.optimization_barrier((parts[-1], whole))
        parts.append(sketch_of(starts[k], gathers[k - n], [whole]))
    return parts


def body(
    inputs,
    out_grads,
    first_moment,
    second_moment,
    signs_in,
    signs_out,
    rows_in,
    rows_out,
    task_ids,
    weights,
):
    width, local_cols = first_moment.shape
    n_col = lax.axis_size("col")
    n_grp = lax.axis_size("grp")
    me_col = lax.axis_index("col")
    left = signed_hadamard(
        rows_in[:, None], jnp.arange(width, dtype=jnp.int32)[None, :], signs_in[None, :]
    )
    offset = me_col * local_cols
    mine = offset + jnp.arange(local_cols, dtype=jnp.int32)
    signs_mine = lax.dynamic_slice_in_dim(signs_out, offset, local_cols, 0)
    right = signed_hadamard(rows_out[None, :], mine[:, None], signs_mine[:, None])
    sixteenth = width // 16
    hops, gathers = [], [8 * sixteenth, 6 * sixteenth, 2 * sixteenth]
    if n_col == 4 * CORES and inputs.shape[1] % 16 == 0:
        hops, gathers = [3 * sixteenth] * 3, [5 * sixteenth, 2 * sixteenth]
    sketch = sum(
        all_sketches(inputs, out_grads, first_moment, second_moment, left, right, hops, gathers)
    )
    examples, n_left, n_right = sketch.shape
    owned = n_left // n_col
    sketch = sketch + lax.ppermute(sketch, "col", [(i, i ^ 1) for i in range(n_col)])
    sketch = sketch.reshape(examples, n_col // 2, 2, owned, n_right)
    sketch = lax.dynamic_index_in_dim(sketch, me_col % 2, 2, keepdims=False)
    sketch = pair_sum(sketch, "col", n_col, 2)
    squares = jnp.sum(sketch * sketch, axis=(1, 2, 3))
    squares = squares + lax.ppermute(squares, "col", [(i, i ^ 1) for i in range(n_col)])
    unit = lax.dynamic_index_in_dim(sketch, me_col // 2, 1, keepdims=False)
    unit = unit * lax.rsqrt(squares / (n_left * n_right) + 1e-06)[:, None, None]
    protos = jnp.arange(PRO_GRP * n_grp, dtype=jnp.int32)
    coef = jnp.where(
        task_ids[:, None] == protos[None, :], weights[:, None].astype(jnp.float32), 0.0
    )
    term = jnp.sum(coef[:, :, None, None] * unit[:, None], axis=0)
    me_grp = lax.axis_index("grp")
    total = lax.dynamic_slice_in_dim(term, me_grp * PRO_GRP, PRO_GRP, 0)
    for d in range(1, n_grp):
        theirs = lax.dynamic_slice_in_dim(term, jnp.bitwise_xor(me_grp, d) * PRO_GRP, PRO_GRP, 0)
        total = total + lax.ppermute(theirs, "grp", [(i, i ^ d) for i in range(n_grp)])
    return total


def solution(mesh):
    placed = (
        P("grp", "col", None),
        P("grp", None, "col"),
        P(None, "col"),
        P(None, "col"),
        P(),
        P(),
        P(),
        P(),
        P("grp"),
        P("grp"),
    )
    return jax.shard_map(
        body, mesh=mesh, in_specs=placed, out_specs=P("grp", "col", None), check_vma=False
    )
```
